512 devices in a mesh: layer: 16 (over y, core), front: 32 (over z, x).
Axes of the slice: x: 4, y: 8, z: 8, core: 2. Of those that a mesh axis runs over, the one named last changes fastest.
Arguments:
- child_rhs: bfloat16 [16, 2, 48, 8192], P('layer', None, None, 'front'), may hold values from -6 to 6
- parent_rhs: bfloat16 [16, 2, 48, 4096], P('layer', None, None, 'front'), may hold values from -6 to 6
- root_rhs: bfloat16 [16, 2, 48, 4096], P('layer', None, None, 'front'), may hold values from -6 to 6
- child_inverse: bfloat16 [16, 2048, 8192], P('layer', None, 'front'), as said below
- child_update: bfloat16 [16, 8192, 2048], P('layer', 'front'), may hold values from -0.125 to 0.125
- parent_inverse: bfloat16 [16, 2048, 4096], P('layer', None, 'front'), as said below
- parent_update: bfloat16 [16, 4096, 3072], P('layer', 'front'), may hold values from -0.125 to 0.125
- root_inverse: bfloat16 [16, 4096, 4096], P('layer', None, 'front'), as said below
- coupling: float32 [16, 4096], P('layer', 'front'), may hold values from 0.25 to 1
- child_map: int32 [4, 2048], replicated, may hold values from 0 to 6143, as said below
- parent_map: int32 [2, 3072], replicated, may hold values from 0 to 4095, as said below
Outputs:
- solution: bfloat16 [16, 2, 48, 4096], P('layer', None, None, 'front')
The draws below stay inside these ranges and needn't reach their ends.
Inputs may be any that keep to these rules, and one draw needn't show every extreme that they name: `child_map`: each row holds 2048 distinct entries; values below 2048 name rows of the parent front's separator, the others name row value - 2048 of the top separator. `parent_map`: each row holds 3072 distinct rows of the top separator. `child_inverse`: each group's matrix, read as rows k and columns f * 2048 + j, is zero where k > j. `parent_inverse`: each group's matrix, read as rows k and columns f * 2048 + j, is zero where k > j. `root_inverse`: each group's matrix is zero below its diagonal.
All inputs are finite; a program needn't handle non-finite values.
Results may differ from the reference program's by a relative error of at most 0.02.
Values may be sent and summed in bfloat16 or wider, within the bound.
A program may use at most 64 MiB of HBM per device.

```python
import math
import jax
import jax.numpy as jnp
from jax import lax

S0 = 4096
S1 = 2048
U1 = 3072
S2 = 2048
U2 = 2048
RHS = 48
GROUPS = 16
N_FRONT = 32


def lower_factor(key, front_count, front_size):
    noise_key, diag_key = jax.random.split(jax.random.fold_in(key, 7))
    shape = (GROUPS, front_size, front_count, front_size)
    noise = jax.random.normal(noise_key, shape, jnp.float32)
    k_index = lax.broadcasted_iota(jnp.int32, (1, front_size, 1, front_size), 1)
    j_index = lax.broadcasted_iota(jnp.int32, (1, front_size, 1, front_size), 3)
    below = (k_index < j_index).astype(jnp.float32)
    on_diag = (k_index == j_index).astype(jnp.float32)
    diag_values = jax.random.uniform(diag_key, (GROUPS, 1, front_count, front_size), jnp.float32, 0.7, 1.3)
    values = noise * below * (0.8 / front_size ** 0.5) + on_diag * diag_values
    return values.reshape(GROUPS, front_size, front_count * front_size).astype(jnp.bfloat16)


def draw_child_inverse(key, part):
    return lower_factor(jax.random.fold_in(key, 21), 4, S2)


def draw_parent_inverse(key, part):
    return lower_factor(jax.random.fold_in(key, 22), 2, S1)


def draw_root_inverse(key, part):
    return lower_factor(jax.random.fold_in(key, 23), 1, S0)


def draw_child_map(key, part):
    keys = jax.random.split(jax.random.fold_in(key, 31), 4)
    return jax.vmap(lambda each_key: jax.random.permutation(each_key, S1 + S0)[:U2])(keys).astype(jnp.int32)


def draw_parent_map(key, part):
    keys = jax.random.split(jax.random.fold_in(key, 32), 2)
    return jax.vmap(lambda each_key: jax.random.permutation(each_key, S0)[:U1])(keys).astype(jnp.int32)


def shard_levels(rng, extent, cuts, low, high):
    gain = 1.0
    for axis_at, blocks in cuts:
        heights = jax.random.uniform(jax.random.fold_in(jax.random.fold_in(rng, 6), axis_at), (blocks,), jnp.float32, low / len(cuts), high / len(cuts))
        gain = gain * jnp.repeat(jnp.exp(heights), extent[axis_at] // blocks).reshape((-1,) + (1,) * (len(extent) - 1 - axis_at))
    return gain


def scatter_about(rng, extent, deviation, bound, pieces=(), held_as=jnp.bfloat16):
    entries = jax.random.normal(rng, extent, jnp.float32) * deviation
    if len(pieces) > 0:
        entries = shard_levels(rng, extent, pieces, -0.22, 0.18) * entries
    return jnp.clip(entries, min=-bound, max=bound).astype(held_as)


def setup_inputs(seed: int = 0) -> dict:
    seeds = jax.random.split(jax.random.key(seed), 12)
    child_rhs = scatter_about(seeds[0], (GROUPS, 2, RHS, 4 * S2), 1.0, 6.0, ((0, 16), (3, 32)))
    parent_rhs = scatter_about(seeds[1], (GROUPS, 2, RHS, 2 * S1), 1.0, 6.0, ((0, 16), (3, 32)))
    root_rhs = scatter_about(seeds[2], (GROUPS, 2, RHS, S0), 1.0, 6.0, ((0, 16), (3, 32)))
    child_inverse = draw_child_inverse(jax.random.fold_in(seeds[11], 71), 0)
    child_update = scatter_about(seeds[4], (GROUPS, 4 * S2, U2), S2 ** -0.5, 0.125, ((0, 16), (1, 32)))
    parent_inverse = draw_parent_inverse(jax.random.fold_in(seeds[11], 71), 0)
    parent_update = scatter_about(seeds[6], (GROUPS, 2 * S1, U1), S1 ** -0.5, 0.125, ((0, 16), (1, 32)))
    root_inverse = draw_root_inverse(jax.random.fold_in(seeds[11], 71), 0)
    coupling = jnp.clip(jnp.exp(math.log(1.0) - 1.3862944 * jax.random.uniform(seeds[8], (GROUPS, S0), jnp.float32) ** shard_levels(seeds[8], (GROUPS, S0), ((0, 16), (1, 32)), -0.2, 0.2)), 0.25, 1.0)
    child_map = draw_child_map(jax.random.fold_in(seeds[11], 71), 0)
    parent_map = draw_parent_map(jax.random.fold_in(seeds[11], 71), 0)
    return dict(child_rhs=child_rhs, parent_rhs=parent_rhs, root_rhs=root_rhs, child_inverse=child_inverse, child_update=child_update, parent_inverse=parent_inverse, parent_update=parent_update, root_inverse=root_inverse, coupling=coupling, child_map=child_map, parent_map=parent_map)


def front_solve(rhs_cols, inverse, front_count):
    row_count = rhs_cols.shape[0]
    front_size = inverse.shape[0]
    blocks = rhs_cols.reshape(row_count, front_count, front_size).astype(jnp.float32)
    factor = inverse.reshape(front_size, front_count, front_size).astype(jnp.float32)
    solved = jnp.einsum("rfk,kfj->rfj", blocks, factor)
    return solved.reshape(row_count, front_count * front_size).astype(jnp.bfloat16)


def share_terms(solved, update):
    row_count = solved.shape[0]
    share_width = solved.shape[1] // N_FRONT
    left_part = solved.reshape(row_count, N_FRONT, share_width).astype(jnp.float32)
    right_part = update.reshape(N_FRONT, share_width, update.shape[1]).astype(jnp.float32)
    return jnp.einsum("rdw,dwu->dru", left_part, right_part)


def place_terms(terms, targets, target_width):
    def place_one(term_block, target_row):
        empty = jnp.zeros((term_block.shape[0], target_width), jnp.float32)
        return empty.at[:, target_row].add(term_block, mode="drop")
    return jax.vmap(place_one)(terms, targets)


def rounded_sum(terms):
    narrow = lax.optimization_barrier(terms.astype(jnp.bfloat16))
    return jnp.sum(narrow.astype(jnp.float32), axis=0)


def group_solve(group_args, child_map, parent_map):
    child_rhs, parent_rhs, root_rhs, incoming, child_inverse, child_update, parent_inverse, parent_update, root_inverse, coupling = group_args
    row_count = child_rhs.shape[0]
    device_ids = jnp.arange(N_FRONT, dtype=jnp.int32)
    child_front = device_ids // (N_FRONT // 4)
    child_targets = child_map[child_front].astype(jnp.int32)
    to_parent = jnp.where(child_targets < S1, (child_front[:, None] // 2) * S1 + child_targets, 2 * S1).astype(jnp.int32)
    to_root = jnp.where(child_targets >= S1, child_targets - S1, S0).astype(jnp.int32)
    child_solved = front_solve(child_rhs, child_inverse, 4)
    child_terms = share_terms(child_solved, child_update)
    parent_sum = rounded_sum(place_terms(child_terms, to_parent, 2 * S1))
    parent_now = (parent_rhs.astype(jnp.float32) - parent_sum).astype(jnp.bfloat16)
    parent_solved = front_solve(parent_now, parent_inverse, 2)
    parent_terms = share_terms(parent_solved, parent_update)
    parent_targets = parent_map[device_ids // (N_FRONT // 2)].astype(jnp.int32)
    root_terms = place_terms(child_terms, to_root, S0) + place_terms(parent_terms, parent_targets, S0)
    share_width = S0 // N_FRONT
    own_cols = (incoming.astype(jnp.float32) - root_rhs.astype(jnp.float32)).reshape(1, row_count, N_FRONT, share_width)
    picker = jnp.eye(N_FRONT, dtype=jnp.float32)
    placed = (picker[:, None, :, None] * own_cols).reshape(N_FRONT, row_count, S0)
    root_now = (-rounded_sum(root_terms + placed)).astype(jnp.bfloat16)
    root_solved = jnp.dot(root_now, root_inverse, preferred_element_type=jnp.float32)
    return root_solved.astype(jnp.bfloat16), (coupling[None, :] * root_solved).astype(jnp.bfloat16)


def reference(child_rhs, parent_rhs, root_rhs, child_inverse, child_update, parent_inverse, parent_update, root_inverse, coupling, child_map, parent_map):
    def run_block(block_id, incoming):
        def per_group(group_args):
            return group_solve(group_args, child_map, parent_map)
        return lax.map(per_group, (child_rhs[:, block_id], parent_rhs[:, block_id], root_rhs[:, block_id], incoming, child_inverse, child_update, parent_inverse, parent_update, root_inverse, coupling))

    silent = jnp.zeros(root_rhs[:, 0].shape, jnp.bfloat16)
    first_sol, outgoing = run_block(0, silent)
    incoming = jnp.concatenate([silent[:1], outgoing[:-1]], axis=0)
    second_sol, leftover = run_block(1, incoming)
    return jnp.stack([first_sol, second_sol], axis=1)
```

```python
import functools

import jax
import jax.numpy as jnp
from jax import lax
from jax.experimental import pallas as pl
from jax.experimental.pallas import tpu as pltpu
from jax.sharding import PartitionSpec as P

BF = jnp.bfloat16
F32 = jnp.float32
MESH = pl.DeviceIdType.MESH

ROWS = 48
W = 128
NX, NZ = 4, 8
NF = NX * NZ
NC, NP = 8, 16
S1 = 2048
S2 = 2048
U1 = 3072
U2 = 2048
S0 = 4096
TN = 512
KC = 256


def one_hot(col_ref, k, first):
    col = col_ref[k * KC : (k + 1) * KC]
    parts = []
    for t in range(TN // W):
        lane = lax.broadcasted_iota(jnp.int32, (KC, W), 1) + (first + t * W)
        parts.append(jnp.where(lane.astype(jnp.int16) == col, BF(1), BF(0)))
    return jnp.concatenate(parts, axis=1)


def placed(rows_refs, col_ref, depth, first):
    sums = [None] * len(rows_refs)
    for k in range(depth // KC):
        hot = one_hot(col_ref, k, first)
        for m, rows in enumerate(rows_refs):
            part = jnp.dot(rows(k * KC, KC), hot, preferred_element_type=F32)
            sums[m] = part if sums[m] is None else sums[m] + part
    return sums


def joined(buf, b, count):
    return jnp.concatenate([buf[b, k] for k in range(count)], axis=1)


def kernel(
    child_rhs, parent_rhs, root_rhs, ci_h, cu_h, pi_h, pu_h, ri_h, coupling_h, cmap_h, pmap_h,
    out,
    ci, cu, pi, pu, ri, coup, cmap, pmap, prhs, rrhs,
    ccol, pcol, cup, pup, c_s, u_s, r_s, root1,
    cbuf, psend, prec, gbuf, xsend, xrec, zsend, zrec, abuf, hsend,
    lsem, csem_s, csem_r, psem_s, psem_r, gsem_s, gsem_r,
    xsem_s, xsem_r, zsem_s, zsem_r, asem_z, asem_f, asem_r,
):
    me = lax.axis_index("front")
    lay = lax.axis_index("layer")
    layers = lax.axis_size("layer")
    z, x = me // NX, me % NX
    i8, i16 = me % NC, me % NP
    b8, b16 = me - i8, me - i16
    has_next = lay < layers - 1
    has_prev = lay > 0

    barrier = pltpu.get_barrier_semaphore()

    def greet(dev):
        pl.semaphore_signal(barrier, inc=1, device_id=dev, device_id_type=MESH)

    @pl.when(has_prev)
    def _():
        @pl.loop(0, z + 1)
        def _(k):
            greet({"layer": lay - 1, "front": k * NX + x})

    for o in (4, 3, 2, 1):
        greet({"front": ((z // 4 * 4 + 4) % NZ + (z + o) % 4) * NX + x})

    @pl.loop(1, NP)
    def _(o):
        greet({"front": b16 + (i16 + o) % NP})

    loads = []

    def load(src, dst):
        copy = pltpu.make_async_copy(src, dst, lsem.at[len(loads)])
        copy.start()
        loads.append(copy)
        return copy

    l_cmap = load(cmap_h, cmap)
    l_cu = load(cu_h.at[0], cu)
    l_child = [load(child_rhs.at[0, b], cbuf.at[b, i8]) for b in range(2)]
    l_pmap = load(pmap_h, pmap)
    l_pu = load(pu_h.at[0], pu)
    l_ci = load(ci_h.at[0], ci)
    l_prhs = load(parent_rhs.at[0], prhs)
    l_pi = load(pi_h.at[0], pi)
    l_rrhs = load(root_rhs.at[0], rrhs)
    l_coup = load(coupling_h, coup)
    l_ri = load(ri_h.at[0], ri)

    @pl.loop(i8 + 1, NC)
    def _(k):
        for b in range(2):
            cbuf[b, k] = jnp.zeros((ROWS, 2 * W), BF)

    @pl.loop(i16 + 1, NP)
    def _(k):
        for b in range(2):
            gbuf[b, k] = jnp.zeros((ROWS, W), BF)

    @pl.loop((z + 1) * NX, NF)
    def _(k):
        for b in range(3):
            abuf[b, k] = jnp.zeros((ROWS, W), BF)

    @pl.when(jnp.logical_not(has_prev))
    def _():
        @pl.loop(0, (z + 1) * NX)
        def _(k):
            abuf[2, k] = jnp.zeros((ROWS, W), BF)

    def columns(map_ref, row, col_ref, count):
        for k in range(count // W):
            targets = map_ref[0:1, k * W : (k + 1) * W]
            for f in range(1, map_ref.shape[0]):
                targets = jnp.where(row == f, map_ref[f : f + 1, k * W : (k + 1) * W], targets)
            col_ref[k * W : (k + 1) * W] = jnp.broadcast_to(targets, (W, W)).T.astype(jnp.int16)

    l_cmap.wait()
    columns(cmap, me // NC, ccol, U2)
    l_cu.wait()

    @pl.loop(0, S1 // TN)
    def _(j):
        halves = [lambda k, n, h=h: cu[h * W : (h + 1) * W, k : k + n] for h in range(2)]
        for h, part in enumerate(placed(halves, ccol, U2, j * TN)):
            cup[j, h * W : (h + 1) * W] = part.astype(BF)

    l_pmap.wait()
    columns(pmap, me // NP, pcol, U1)

    for copy in l_child:
        copy.wait()
    pl.semaphore_wait(barrier, NP - 1 + 4 + jnp.where(has_next, NZ - z, 0))

    def send(src, dst, s_sem, r_sem, dev):
        return pltpu.make_async_remote_copy(
            src_ref=src, dst_ref=dst, send_sem=s_sem, recv_sem=r_sem, device_id=dev, device_id_type=MESH
        )

    def child_copy(b, to, slot):
        return send(
            cbuf.at[b, slot], cbuf.at[b, slot], csem_s.at[b, to], csem_r.at[b, slot], {"front": b8 + to}
        )

    for b in range(2):
        @pl.loop(i8 + 1, NC)
        def _(k):
            child_copy(b, k, i8).start()

    l_pu.wait()

    @pl.loop(0, NZ)
    def _(j):
        whole = [lambda k, n: pu[:, k : k + n]]
        pup[j] = placed(whole, pcol, U1, j * TN)[0].astype(BF)

    def parent_copy(b, to, slot):
        return send(
            psend.at[b, to], prec.at[b, slot], psem_s.at[b, to], psem_r.at[b, slot], {"front": b16 + to}
        )

    l_ci.wait()
    for b in range(2):
        @pl.loop(0, i8)
        def _(k):
            child_copy(b, i8, k).wait_recv()

        solved = jnp.dot(joined(cbuf, b, NC), ci[...], preferred_element_type=F32).astype(BF)
        c_s[b * ROWS : (b + 1) * ROWS] = solved
        for j in range(S1 // TN):
            terms = jnp.dot(solved, cup[j], preferred_element_type=F32).astype(BF)
            for t in range(TN // W):
                psend[b, j * (TN // W) + t] = terms[:, t * W : (t + 1) * W]

        @pl.loop(1, NP)
        def _(o):
            parent_copy(b, (i16 + o) % NP, i16).start()

    for j in range(U2 // TN):
        u_s[:, j * TN : (j + 1) * TN] = jnp.dot(
            c_s[...], cu[:, j * TN : (j + 1) * TN], preferred_element_type=F32
        ).astype(BF)

    @pl.loop(0, NZ)
    def _(j):
        whole = [lambda k, n: u_s[:, k : k + n]]
        r_s[j] = placed(whole, ccol, U2, S1 + j * TN)[0]

    def gather_copy(b, to, slot):
        return send(
            gbuf.at[b, slot], gbuf.at[b, slot], gsem_s.at[b, to], gsem_r.at[b, slot], {"front": b16 + to}
        )

    l_prhs.wait()
    for b in range(2):
        @pl.loop(1, NP)
        def _(o):
            parent_copy(b, i16, (i16 + o) % NP).wait_recv()

        prec[b, i16] = psend[b, i16]
        total = prec[b, 0].astype(F32)
        for k in range(1, NP):
            total += prec[b, k].astype(F32)
        gbuf[b, i16] = (prhs[b].astype(F32) - total).astype(BF)

        @pl.loop(i16 + 1, NP)
        def _(k):
            gather_copy(b, k, i16).start()

    def row_of(s):
        return (z + s + 2) % NZ

    def x_copy(b, half, p):
        to = (x + p) % NX
        part = pl.ds(half * 4, 4)
        return send(
            xsend.at[b, to, part], xrec.at[b, x, part],
            xsem_s.at[b, half, p], xsem_r.at[b, half, x], {"front": z * NX + to},
        )

    def x_arrival(b, half, p):
        frm = (x + p) % NX
        part = pl.ds(half * 4, 4)
        return send(
            xsend.at[b, x, part], xrec.at[b, frm, part],
            xsem_s.at[b, half, p], xsem_r.at[b, half, frm], {"front": me},
        )

    l_pi.wait()
    for b in range(2):
        @pl.loop(0, i16)
        def _(k):
            gather_copy(b, i16, k).wait_recv()

        solved = jnp.dot(joined(gbuf, b, NP), pi[...], preferred_element_type=F32).astype(BF)
        for half in range(2):
            for s in range(half * 4, half * 4 + 4):
                row = row_of(s)
                terms = jnp.dot(solved, pup[row], preferred_element_type=F32)
                terms = (terms + r_s[row, b * ROWS : (b + 1) * ROWS]).astype(BF)
                for t in range(NX):
                    xsend[b, t, s] = terms[:, t * W : (t + 1) * W]
            for p in (2, 1, 3):
                x_copy(b, half, p).start()

    def z_copy(b, s):
        row = row_of(s)
        return send(
            zsend.at[b, s], zrec.at[b, z], zsem_s.at[b, s], zsem_r.at[b, z], {"front": row * NX + x}
        )

    def sum_x(b):
        for half in range(2):
            for p in (1, 3, 2):
                x_arrival(b, half, p).wait_recv()
            for s in range(half * 4, half * 4 + 4):
                total = xsend[b, x, s].astype(F32)
                for p in (1, 2, 3):
                    total += xrec[b, (x + p) % NX, s].astype(F32)
                zsend[b, s] = total.astype(BF)
                if s != 6:
                    z_copy(b, s).start()

    def row_copy(a, o, src, dev):
        return send(src, abuf.at[a, me], asem_z.at[a, o], asem_r.at[a, me], dev)

    def row_arrival(a, o, slot):
        return send(abuf.at[a, slot], abuf.at[a, slot], asem_z.at[a, o], asem_r.at[a, slot], {"front": me})

    def pass_on(a, o, p):
        slot = me - NX * o
        return send(
            abuf.at[a, slot], abuf.at[a, slot], asem_f.at[a, NX * o + p], asem_r.at[a, slot],
            {"front": z * NX + (x + p) % NX},
        )

    def sum_z(b):
        for o in range(1, NZ):
            frm = (z + o) % NZ
            send(
                zsend.at[b, 6], zrec.at[b, frm], zsem_s.at[b, 0], zsem_r.at[b, frm], {"front": me}
            ).wait_recv()
        total = zsend[b, 6].astype(F32)
        for o in range(1, NZ):
            total += zrec[b, (z + o) % NZ].astype(F32)
        abuf[b, me] = (rrhs[b].astype(F32) - total).astype(BF)
        for o in (4, 3, 5, 2, 6, 1, 7):
            @pl.when(z + o < NZ)
            def _():
                row_copy(b, o, abuf.at[b, me], {"front": me + NX * o}).start()
        for p in (2, 1, 3):
            pass_on(b, 0, p).start()

    def pass_rows(a, offsets):
        for o in offsets:
            @pl.when(z >= o)
            def _():
                row_arrival(a, o, me - NX * o).wait_recv()
                for p in (2, 1, 3):
                    pass_on(a, o, p).start()

    def wait_passed(a):
        for o in range(NZ):
            @pl.when(z >= o)
            def _():
                for p in (1, 2, 3):
                    row_arrival(a, o, (z - o) * NX + (x + p) % NX).wait_recv()

    far = (1, 7, 2, 6, 3, 5, 4)

    def root_solve(a):
        return jnp.dot(joined(abuf, a, NF), ri[...], preferred_element_type=F32)

    l_rrhs.wait()
    sum_x(0)
    sum_z(0)
    sum_x(1)
    pass_rows(0, far)
    sum_z(1)
    l_coup.wait()
    l_ri.wait()
    wait_passed(0)
    solved = root_solve(0)
    hsend[...] = (coup[...] * solved).astype(BF)

    @pl.when(has_next)
    def _():
        for o in (4, 3, 5, 2, 6, 1, 7, 0):
            @pl.when(z + o < NZ)
            def _():
                row_copy(2, o, hsend, {"layer": lay + 1, "front": me + NX * o}).start()

    out[0, 0] = solved.astype(BF)
    pass_rows(1, far)

    @pl.when(has_prev)
    def _():
        pass_rows(2, (0,) + far)

    wait_passed(1)
    root1[...] = root_solve(1)

    @pl.when(has_prev)
    def _():
        wait_passed(2)

    out[0, 1] = (root1[...] - root_solve(2)).astype(BF)

    for b in range(2):
        @pl.loop(i8 + 1, NC)
        def _(k):
            child_copy(b, k, i8).wait_send()

        @pl.loop(1, NP)
        def _(o):
            parent_copy(b, (i16 + o) % NP, i16).wait_send()

        @pl.loop(i16 + 1, NP)
        def _(k):
            gather_copy(b, k, i16).wait_send()

        for half in range(2):
            for p in (1, 2, 3):
                x_copy(b, half, p).wait_send()
        for s in range(NZ):
            if s != 6:
                z_copy(b, s).wait_send()

        @pl.loop(1, NZ - z)
        def _(o):
            row_copy(b, o, abuf.at[b, me], {"front": me + NX * o}).wait_send()

        @pl.loop(0, z + 1)
        def _(o):
            for p in (1, 2, 3):
                pass_on(b, o, p).wait_send()

    @pl.when(has_next)
    def _():
        @pl.loop(0, NZ - z)
        def _(o):
            row_copy(2, o, hsend, {"layer": lay + 1, "front": me + NX * o}).wait_send()

    @pl.when(has_prev)
    def _():
        @pl.loop(0, z + 1)
        def _(o):
            for p in (1, 2, 3):
                pass_on(2, o, p).wait_send()


def body(*args):
    piece = (ROWS, W)
    dma = pltpu.SemaphoreType.DMA
    scratch = [
        pltpu.VMEM((S2, 256), BF), pltpu.VMEM((256, U2), BF), pltpu.VMEM((S1, W), BF),
        pltpu.VMEM((W, U1), BF), pltpu.VMEM((S0, W), BF), pltpu.VMEM((1, W), F32),
        pltpu.VMEM((4, U2), jnp.int32), pltpu.VMEM((2, U1), jnp.int32),
        pltpu.VMEM((2, *piece), BF), pltpu.VMEM((2, *piece), BF),
        pltpu.VMEM((U2, W), jnp.int16), pltpu.VMEM((U1, W), jnp.int16),
        pltpu.VMEM((S1 // TN, 256, TN), BF), pltpu.VMEM((NZ, W, TN), BF),
        pltpu.VMEM((2 * ROWS, 256), BF), pltpu.VMEM((2 * ROWS, U2), BF),
        pltpu.VMEM((NZ, 2 * ROWS, TN), F32), pltpu.VMEM(piece, F32),
        pltpu.VMEM((2, NC, ROWS, 256), BF),
        pltpu.VMEM((2, NP, *piece), BF), pltpu.VMEM((2, NP, *piece), BF), pltpu.VMEM((2, NP, *piece), BF),
        pltpu.VMEM((2, NX, NZ, *piece), BF), pltpu.VMEM((2, NX, NZ, *piece), BF),
        pltpu.VMEM((2, NZ, *piece), BF), pltpu.VMEM((2, NZ, *piece), BF),
        pltpu.VMEM((3, NF, *piece), BF), pltpu.VMEM(piece, BF),
        dma((11 + 1,)), dma((2, NC)), dma((2, NC)), dma((2, NP)), dma((2, NP)), dma((2, NP)), dma((2, NP)),
        dma((2, 2, NX)), dma((2, 2, NX)), dma((2, NZ)), dma((2, NZ)),
        dma((3, NZ)), dma((3, NF)), dma((3, NF)),
    ]
    return pl.pallas_call(
        kernel,
        out_shape=jax.ShapeDtypeStruct((1, 2, ROWS, W), BF),
        in_specs=[pl.BlockSpec(memory_space=pl.ANY)] * 11,
        out_specs=pl.BlockSpec(memory_space=pltpu.VMEM),
        scratch_shapes=scratch,
        compiler_params=pltpu.CompilerParams(
            collective_id=0, has_side_effects=True, vmem_limit_bytes=40 * 2**20
        ),
    )(*args)


def solution(mesh):
    placed_as = (
        P("layer", None, None, "front"),
        P("layer", None, None, "front"),
        P("layer", None, None, "front"),
        P("layer", None, "front"),
        P("layer", "front", None),
        P("layer", None, "front"),
        P("layer", "front", None),
        P("layer", None, "front"),
        P("layer", "front"),
        P(),
        P(),
    )
    return jax.shard_map(
        body, mesh=mesh, in_specs=placed_as, out_specs=P("layer", None, None, "front"), check_vma=False
    )
```
